32 devices in a mesh: row: 4 (over y, core), col: 8 (over z, x).
Axes of the slice: x: 2, y: 2, z: 4, core: 2. Of those that a mesh axis runs over, the one named last changes fastest.
Arguments:
- row_points: float32 [64, 8192], P(None, 'row'), may hold values from -6 to 6
- panel_points: float32 [64, 1024], P(None, 'col'), may hold values from -6 to 6
- scales: float32 [64], replicated, may hold values from 0.005 to 0.03
Outputs:
- diag_factor: float32 [1024, 1024], P('row', 'col')
- panel_factor_t: float32 [1024, 8192], P('col', 'row')
- updated_ahead_t: float32 [1024, 8192], P('col', 'row')
The draws below stay inside these ranges and needn't reach their ends.
All inputs are finite; a program needn't handle non-finite values.
Results may differ from the reference program's by a relative error of at most 0.0003.
Values sent between devices are 32-bit elements; how exact they have to be, the bound alone decides.
A program may use at most 128 MiB of HBM per device.

```python
import math
import jax
import jax.numpy as jnp
from jax import lax

F = 64
B = 1024
M = 8192


def block_levels(key, dims, pieces, least, largest):
    loudness = 1.0
    for position, blocks in pieces:
        draws = jax.random.uniform(jax.random.fold_in(jax.random.fold_in(key, 6), position), (blocks,), jnp.float32, least / len(pieces), largest / len(pieces))
        loudness = loudness * jnp.repeat(jnp.exp(draws), dims[position] // blocks).reshape((-1,) + (1,) * (len(dims) - 1 - position))
    return loudness


def scatter_about(own_key, extent, spread, limit, pieces=(), kind=jnp.bfloat16):
    result = jax.random.normal(own_key, extent, jnp.float32) * spread
    if len(pieces) > 0:
        result = block_levels(own_key, extent, pieces, -0.22, 0.18) * result
    return jnp.clip(result, min=-limit, max=limit).astype(kind)


def setup_inputs(seed: int = 0) -> dict:
    streams_of = jax.random.split(jax.random.key(seed), 4)
    return {
        "row_points": scatter_about(streams_of[0], (F, M), 1.0, 6.0, ((1, 4),), jnp.float32),
        "panel_points": scatter_about(streams_of[1], (F, B), 1.0, 6.0, ((1, 8),), jnp.float32),
        "scales": jnp.clip(jnp.exp(jax.random.uniform(streams_of[2], (F,), jnp.float32, math.log(0.005), math.log(0.03))), 0.005, 0.03),
    }


RIDGE = 0.5

def kernel_block(sources, targets, scales):
    weighted = sources * scales[:, None]
    source_sq = jnp.sum(weighted * sources, axis=0)
    target_sq = jnp.sum(targets * targets * scales[:, None], axis=0)
    cross = lax.dot_general(weighted.astype(jnp.float32), targets.astype(jnp.float32), (((0,), (0,)), ((), ())), precision=lax.Precision.HIGHEST, preferred_element_type=jnp.float32)
    return jnp.exp(2.0 * cross - source_sq[:, None] - target_sq[None, :])

def reference(row_points, panel_points, scales):
    diag_block = kernel_block(panel_points, panel_points, scales) + RIDGE * jnp.eye(B, dtype=jnp.float32)
    diag_factor = jnp.linalg.cholesky(diag_block)
    panel_kernel = kernel_block(panel_points, row_points, scales)
    panel_factor = lax.linalg.triangular_solve(diag_factor, panel_kernel, left_side=True, lower=True)
    look_points = row_points[:, :B]
    cross_term = lax.dot_general(panel_factor[:, :B].astype(jnp.float32), panel_factor.astype(jnp.float32), (((0,), (0,)), ((), ())), precision=lax.Precision.HIGHEST, preferred_element_type=jnp.float32)
    updated = kernel_block(look_points, row_points, scales) - cross_term
    return (diag_factor, panel_factor, updated)
```

```python
import functools

import jax
import jax.numpy as jnp
from jax import lax
from jax.experimental import pallas as pl
from jax.experimental.pallas import tpu as pltpu
from jax.sharding import PartitionSpec as P

RIDGE = 0.5
BLK = 128
TILE = 256
F32 = jnp.float32
BF16 = jnp.bfloat16


def gather_kernel(n_row, n_col, root, pan_ref, look_ref, g_ref, lk_ref, send, recv, lsend, lrecv, own):
    row = lax.axis_index("row")
    col = lax.axis_index("col")
    barrier = pltpu.get_barrier_semaphore()
    for d in range(1, n_col):
        pl.semaphore_signal(
            barrier, inc=1, device_id=(row, lax.rem(col + d, n_col)), device_id_type=pl.DeviceIdType.MESH
        )
    for d in range(1, n_row):
        pl.semaphore_signal(
            barrier, inc=1, device_id=(lax.rem(row + d, n_row), col), device_id_type=pl.DeviceIdType.MESH
        )
    pl.semaphore_wait(barrier, n_col + n_row - 2)

    def panel_copy(d):
        return pltpu.make_async_remote_copy(
            src_ref=pan_ref,
            dst_ref=g_ref.at[col],
            send_sem=send.at[d],
            recv_sem=recv.at[d],
            device_id=(row, lax.rem(col + d, n_col)),
            device_id_type=pl.DeviceIdType.MESH,
        )

    def panel_arrival(d):
        return pltpu.make_async_remote_copy(
            src_ref=pan_ref,
            dst_ref=g_ref.at[lax.rem(col + n_col - d, n_col)],
            send_sem=send.at[d],
            recv_sem=recv.at[d],
            device_id=(row, lax.rem(col + d, n_col)),
            device_id_type=pl.DeviceIdType.MESH,
        )

    def look_copy(d):
        return pltpu.make_async_remote_copy(
            src_ref=look_ref,
            dst_ref=lk_ref,
            send_sem=lsend.at[d],
            recv_sem=lrecv,
            device_id=(lax.rem(row + d, n_row), col),
            device_id_type=pl.DeviceIdType.MESH,
        )

    @pl.when(row == root)
    def _():
        for d in range(1, n_row):
            look_copy(d).start()

    for d in range(1, n_col):
        panel_copy(d).start()
    mine = pltpu.make_async_copy(pan_ref, g_ref.at[col], own.at[0])
    mine.start()

    @pl.when(row == root)
    def _():
        keep = pltpu.make_async_copy(look_ref, lk_ref, own.at[1])
        keep.start()
        keep.wait()
        for d in range(1, n_row):
            look_copy(d).wait_send()

    @pl.when(row != root)
    def _():
        look_copy(1).wait_recv()

    mine.wait()
    for d in range(1, n_col):
        panel_copy(d).wait_send()
        panel_arrival(d).wait_recv()


def gather_points(panel_points, local_look, n_row, n_col, root):
    feats, share = panel_points.shape
    vmem = pl.BlockSpec(memory_space=pltpu.VMEM)
    return pl.pallas_call(
        functools.partial(gather_kernel, n_row, n_col, root),
        out_shape=(
            jax.ShapeDtypeStruct((n_col, feats, share), F32),
            jax.ShapeDtypeStruct((feats, share), F32),
        ),
        in_specs=[vmem, vmem],
        out_specs=(vmem, vmem),
        scratch_shapes=[
            pltpu.SemaphoreType.DMA((n_col,)),
            pltpu.SemaphoreType.DMA((n_col,)),
            pltpu.SemaphoreType.DMA((n_row,)),
            pltpu.SemaphoreType.DMA,
            pltpu.SemaphoreType.DMA((2,)),
        ],
        compiler_params=pltpu.CompilerParams(collective_id=0, has_side_effects=True),
        name="gather_points",
    )(panel_points, local_look)


def split(x):
    hi = x.astype(BF16)
    return hi, (x - hi.astype(F32)).astype(BF16)


def parts3(x):
    a = x.astype(BF16).astype(F32)
    b = (x - a).astype(BF16).astype(F32)
    return a, b, (x - a) - b


def dot(a, b):
    return jnp.dot(a, b, preferred_element_type=F32)


def dot_t(a, b):
    return lax.dot_general(a, b, (((0,), (0,)), ((), ())), preferred_element_type=F32)


def product(mul, ah, al, bh, bl):
    return mul(ah, bh) + (mul(ah, bl) + mul(al, bh))


def stacked(points, scales, left):
    feats, n = points.shape
    weighted = points * scales
    norm = jnp.sum(weighted * points, axis=0, keepdims=True)
    main = 2.0 * weighted if left else points
    hi = main.astype(BF16).astype(F32)
    lo = main - hi
    n0, n1, n2 = (jnp.broadcast_to(-p, (feats, n)) for p in parts3(norm))
    place = lax.broadcasted_iota(jnp.int32, (feats, n), 0)
    first = 0 if left else 3
    ones = jnp.where((place >= 3 - first) & (place < 6 - first), 1.0, 0.0)
    tail = jnp.where(
        place == first, n0, jnp.where(place == first + 1, n1, jnp.where(place == first + 2, n2, ones))
    )
    blocks = [hi, lo, hi, tail] if left else [hi, hi, lo, tail]
    return jnp.concatenate(blocks, axis=0)


def lanes(x, c):
    return jnp.broadcast_to(x[:, c : c + 1], (8, BLK))


def rows(x, j):
    return jnp.broadcast_to(x[j : j + 1, :], (8, BLK))


def reciprocal(p):
    q = pl.reciprocal(p, approx=True)
    e = 1.0 - p * q
    return q + q * (e + e * e)


def factor_block(block):
    n = BLK // 8
    sub = lax.broadcasted_iota(jnp.int32, (8, BLK), 0)
    lane = lax.broadcasted_iota(jnp.int32, (8, BLK), 1)
    t = [block[8 * r : 8 * r + 8, :] for r in range(n)]
    s = [jnp.where(lane == sub + 8 * r, 1.0, 0.0).astype(F32) for r in range(n)]
    for k in range(n):
        top, side = t[k], s[k]
        v = [lanes(top, 8 * k + j) for j in range(8)]
        mult = []
        diag = jnp.ones((8, BLK), F32)
        for j in range(8):
            across = [rows(v[m], j) for m in range(8)]
            p = across[j]
            q = reciprocal(p)
            vj = v[j]
            mult.append(jnp.where(sub > j, vj * q, 0.0))
            diag = jnp.where(sub == j, p, diag)
            vp = jnp.where(sub == j, vj - 1.0, vj)
            unit = jnp.where(sub == j, 1.0, 0.0)
            v = [unit - vp * q if m == j else v[m] - (vp * across[m]) * q for m in range(8)]
        wt = functools.reduce(jnp.add, [v[j] * rows(top, j) for j in range(8)])
        ws = functools.reduce(jnp.add, [v[j] * rows(side, j) for j in range(8)])
        wtr = [rows(wt, j) for j in range(8)]
        wsr = [rows(ws, j) for j in range(8)]
        for r in range(k + 1, n):
            c = [lanes(t[r], 8 * k + j) for j in range(8)]
            t[r] = t[r] - functools.reduce(jnp.add, [c[j] * wtr[j] for j in range(8)])
            s[r] = s[r] - functools.reduce(jnp.add, [c[j] * wsr[j] for j in range(8)])
        for j in range(7):
            top = top - mult[j] * rows(top, j)
            side = side - mult[j] * rows(side, j)
        root = lax.rsqrt(diag)
        root = root * (1.5 - 0.5 * diag * root * root)
        t[k] = jnp.where(lane >= sub + 8 * k, top * root, 0.0)
        s[k] = side * root
    return jnp.concatenate(t, axis=0), jnp.concatenate(s, axis=0)


def panel_kernel(
    share, pan_ref, look_ref, rows_ref, sc_ref, u_out, panel_out, ahead_out,
    lhs, a, uh, ul, ih, il, work, y, yh, yl, zh, zl,
):
    b = pan_ref.shape[1]
    n_blk = b // BLK
    wide = b + BLK
    col = lax.axis_index("col")
    first = col * share
    home = first // BLK
    scales = sc_ref[...]
    lhs[...] = stacked(pan_ref[...], scales, True).T.astype(BF16)
    look_lhs = stacked(look_ref[...], scales, True).T.astype(BF16)

    def entries(pts):
        return jnp.exp(dot(lhs[...], stacked(pts, scales, False).astype(BF16)))

    for c in range(0, b, TILE):
        at_row = lax.broadcasted_iota(jnp.int32, (b, TILE), 0)
        at_col = lax.broadcasted_iota(jnp.int32, (b, TILE), 1) + c
        a[:, c : c + TILE] = entries(pan_ref[:, c : c + TILE]) + jnp.where(at_row == at_col, RIDGE, 0.0)
    a[:, b:wide] = entries(look_ref[...])

    @pl.loop(0, n_blk)
    def _(kb):
        o = pl.multiple_of(kb * BLK, BLK)
        for i in range(n_blk):

            @pl.when(kb == i)
            def _(i=i):
                s = i * BLK
                cur = a[s : s + BLK, s:wide]
                if i > 0:
                    cur = cur - product(
                        dot_t, uh[:s, s : s + BLK], ul[:s, s : s + BLK], uh[:s, s:wide], ul[:s, s:wide]
                    )
                work[:, :BLK] = cur[:, :BLK]
                a[s : s + BLK, s:wide] = cur

        upper, inverse = factor_block(work[:, :BLK])
        inv_h, inv_l = split(inverse)
        ih[pl.ds(o, BLK), :] = inv_h
        il[pl.ds(o, BLK), :] = inv_l
        for i in range(n_blk):

            @pl.when(kb == i)
            def _(i=i):
                s = i * BLK
                rest = a[s : s + BLK, s + BLK : wide]
                rh, rl = split(rest)
                done = product(dot, inv_h, inv_l, rh, rl)
                a[s : s + BLK, s + BLK : wide] = done
                dh, dl = split(done)
                uh[s : s + BLK, s + BLK : wide] = dh
                ul[s : s + BLK, s + BLK : wide] = dl

        a[pl.ds(o, BLK), pl.ds(o, BLK)] = upper

    at_row = lax.broadcasted_iota(jnp.int32, (BLK, BLK), 0)
    at_col = lax.broadcasted_iota(jnp.int32, (BLK, BLK), 1)
    unit = jnp.where(at_row == at_col, 1.0, 0.0).astype(F32)
    for i in reversed(range(n_blk)):
        s = i * BLK
        right = jnp.concatenate([jnp.where(home == i, unit, 0.0), a[s : s + BLK, b:wide]], axis=1)
        if i < n_blk - 1:
            e = s + BLK
            right = right - product(dot, uh[s:e, e:b], ul[s:e, e:b], yh[e:, :], yl[e:, :])
        rh, rl = split(right)
        done = product(dot_t, ih[s : s + BLK, :], il[s : s + BLK, :], rh, rl)
        y[s : s + BLK, :] = done
        dh, dl = split(done)
        yh[s : s + BLK, :] = dh
        yl[s : s + BLK, :] = dl
    th, tl = split(y[...].T)
    zh[...] = th
    zl[...] = tl

    inner = pl.multiple_of(lax.rem(first, BLK), min(share, BLK))

    @pl.loop(0, rows_ref.shape[1] // TILE)
    def _(step):
        at = pl.ds(pl.multiple_of(step * TILE, TILE), TILE)
        pts = stacked(rows_ref[:, at], scales, False).astype(BF16)
        kh, kl = split(jnp.exp(dot(lhs[...], pts)))
        both = product(dot, zh[...], zl[...], kh, kl)
        ahead = jnp.exp(dot(look_lhs, pts)) - both[BLK:, :]
        if share == BLK:
            panel_out[:, at] = both[:BLK, :]
            ahead_out[:, at] = ahead
        else:
            work[:, :TILE] = both[:BLK, :]
            panel_out[:, at] = work[pl.ds(inner, share), :TILE]
            ahead_out[:, at] = ahead[:share, :]

    u_rows = u_out.shape[1]
    u_out[...] = a[
        pl.ds(pl.multiple_of(first, share), share),
        pl.ds(pl.multiple_of(lax.axis_index("row") * u_rows, BLK), u_rows),
    ]


def panel_step(panel, look, row_points, scales, share, row_share):
    feats, b = panel.shape
    rows_dev = row_points.shape[1]
    wide = b + BLK
    vmem = pl.BlockSpec(memory_space=pltpu.VMEM)
    return pl.pallas_call(
        functools.partial(panel_kernel, share),
        out_shape=(
            jax.ShapeDtypeStruct((share, row_share), F32),
            jax.ShapeDtypeStruct((share, rows_dev), F32),
            jax.ShapeDtypeStruct((share, rows_dev), F32),
        ),
        in_specs=[vmem] * 4,
        out_specs=(vmem,) * 3,
        scratch_shapes=[
            pltpu.VMEM((b, 4 * feats), BF16),
            pltpu.VMEM((b, wide), F32),
            pltpu.VMEM((b, wide), BF16),
            pltpu.VMEM((b, wide), BF16),
            pltpu.VMEM((b, BLK), BF16),
            pltpu.VMEM((b, BLK), BF16),
            pltpu.VMEM((BLK, TILE), F32),
            pltpu.VMEM((b, 2 * BLK), F32),
            pltpu.VMEM((b, 2 * BLK), BF16),
            pltpu.VMEM((b, 2 * BLK), BF16),
            pltpu.VMEM((2 * BLK, b), BF16),
            pltpu.VMEM((2 * BLK, b), BF16),
        ],
        compiler_params=pltpu.CompilerParams(vmem_limit_bytes=48 * 1024 * 1024),
        name="panel_step",
    )(panel, look, row_points, scales[:, None])


def body(row_points, panel_points, scales):
    n_col = lax.axis_size("col")
    n_row = lax.axis_size("row")
    col_index = lax.axis_index("col")
    row_index = lax.axis_index("row")
    feats, share = panel_points.shape
    b = share * n_col
    row_share = b // n_row
    rows_dev = row_points.shape[1]
    assert b <= rows_dev and BLK % share == 0
    first_col = col_index * share
    local_look = lax.dynamic_slice_in_dim(row_points, first_col, share, 1)
    gathered, look = gather_points(panel_points, local_look, n_row, n_col, 0)
    panel = jnp.transpose(gathered, (1, 0, 2)).reshape(feats, b)
    look = jnp.pad(look, ((0, 0), (0, BLK - share)))
    u_tile, panel_tile, updated = panel_step(panel, look, row_points, scales, share, row_share)
    at_row = lax.broadcasted_iota(jnp.int32, (row_share, share), 0) + row_index * row_share
    at_col = lax.broadcasted_iota(jnp.int32, (row_share, share), 1) + first_col
    diag_tile = jnp.where(at_row >= at_col, u_tile.T, 0.0)
    return (diag_tile, panel_tile, updated)


def solution(mesh):
    return jax.shard_map(
        body,
        mesh=mesh,
        in_specs=(P(None, "row"), P(None, "col"), P()),
        out_specs=(P("row", "col"), P("col", "row"), P("col", "row")),
        check_vma=False,
    )
```

```python
import functools

import jax
import jax.numpy as jnp
from jax import lax
from jax.experimental import pallas as pl
from jax.experimental.pallas import tpu as pltpu
from jax.sharding import PartitionSpec as P

RIDGE = 0.5
BLK = 128
TILE = 256
F32 = jnp.float32
BF16 = jnp.bfloat16


def gather_kernel(n_row, n_col, root, pan_ref, look_ref, g_ref, lk_ref, send, recv, lsend, lrecv, own):
    row = lax.axis_index("row")
    col = lax.axis_index("col")
    share = pan_ref.shape[1]
    aligned = share % BLK == 0

    def slot(c):
        if aligned:
            return g_ref.at[:, pl.ds(pl.multiple_of(c * share, share), share)]
        return g_ref.at[c]

    look_src = look_ref.at[:, pl.ds(pl.multiple_of(col * share, share), share)] if aligned else look_ref
    barrier = pltpu.get_barrier_semaphore()
    for d in range(1, n_col):
        pl.semaphore_signal(
            barrier, inc=1, device_id=(row, lax.rem(col + d, n_col)), device_id_type=pl.DeviceIdType.MESH
        )
    for d in range(1, n_row):
        pl.semaphore_signal(
            barrier, inc=1, device_id=(lax.rem(row + d, n_row), col), device_id_type=pl.DeviceIdType.MESH
        )
    pl.semaphore_wait(barrier, n_col + n_row - 2)

    def panel_copy(d):
        return pltpu.make_async_remote_copy(
            src_ref=pan_ref,
            dst_ref=slot(col),
            send_sem=send.at[d],
            recv_sem=recv.at[d],
            device_id=(row, lax.rem(col + d, n_col)),
            device_id_type=pl.DeviceIdType.MESH,
        )

    def panel_arrival(d):
        return pltpu.make_async_remote_copy(
            src_ref=pan_ref,
            dst_ref=slot(lax.rem(col + n_col - d, n_col)),
            send_sem=send.at[d],
            recv_sem=recv.at[d],
            device_id=(row, lax.rem(col + d, n_col)),
            device_id_type=pl.DeviceIdType.MESH,
        )

    def look_copy(d):
        return pltpu.make_async_remote_copy(
            src_ref=look_src,
            dst_ref=lk_ref,
            send_sem=lsend.at[d],
            recv_sem=lrecv,
            device_id=(lax.rem(row + d, n_row), col),
            device_id_type=pl.DeviceIdType.MESH,
        )

    @pl.when(row == root)
    def _():
        for d in range(1, n_row):
            look_copy(d).start()

    for d in range(1, n_col):
        panel_copy(d).start()
    mine = pltpu.make_async_copy(pan_ref, slot(col), own.at[0])
    mine.start()

    @pl.when(row == root)
    def _():
        keep = pltpu.make_async_copy(look_src, lk_ref, own.at[1])
        keep.start()
        keep.wait()
        for d in range(1, n_row):
            look_copy(d).wait_send()

    @pl.when(row != root)
    def _():
        look_copy(1).wait_recv()

    mine.wait()
    for d in range(1, n_col):
        panel_copy(d).wait_send()
        panel_arrival(d).wait_recv()


def gather_points(panel_points, local_look, n_row, n_col, root):
    feats, share = panel_points.shape
    vmem = pl.BlockSpec(memory_space=pltpu.VMEM)
    return pl.pallas_call(
        functools.partial(gather_kernel, n_row, n_col, root),
        out_shape=(
            jax.ShapeDtypeStruct((feats, n_col * share) if share % BLK == 0 else (n_col, feats, share), F32),
            jax.ShapeDtypeStruct((feats, share), F32),
        ),
        in_specs=[vmem, pl.BlockSpec(memory_space=pl.ANY) if share % BLK == 0 else vmem],
        out_specs=(vmem, vmem),
        scratch_shapes=[
            pltpu.SemaphoreType.DMA((n_col,)),
            pltpu.SemaphoreType.DMA((n_col,)),
            pltpu.SemaphoreType.DMA((n_row,)),
            pltpu.SemaphoreType.DMA,
            pltpu.SemaphoreType.DMA((2,)),
        ],
        compiler_params=pltpu.CompilerParams(collective_id=0, has_side_effects=True),
        name="gather_points",
    )(panel_points, local_look)


def split(x):
    hi = x.astype(BF16)
    return hi, (x - hi.astype(F32)).astype(BF16)


def parts3(x):
    a = x.astype(BF16).astype(F32)
    b = (x - a).astype(BF16).astype(F32)
    return a, b, (x - a) - b


def dot(a, b):
    return jnp.dot(a, b, preferred_element_type=F32)


def dot_t(a, b):
    return lax.dot_general(a, b, (((0,), (0,)), ((), ())), preferred_element_type=F32)


def product(mul, ah, al, bh, bl):
    return mul(ah, bh) + (mul(ah, bl) + mul(al, bh))


def stacked(points, scales, left):
    feats, n = points.shape
    weighted = points * scales
    norm = jnp.sum(weighted * points, axis=0, keepdims=True)
    main = 2.0 * weighted if left else points
    hi = main.astype(BF16).astype(F32)
    lo = main - hi
    n0, n1, n2 = (jnp.broadcast_to(-p, (feats, n)) for p in parts3(norm))
    place = lax.broadcasted_iota(jnp.int32, (feats, n), 0)
    first = 0 if left else 3
    ones = jnp.where((place >= 3 - first) & (place < 6 - first), 1.0, 0.0)
    tail = jnp.where(
        place == first, n0, jnp.where(place == first + 1, n1, jnp.where(place == first + 2, n2, ones))
    )
    blocks = [hi, lo, hi, tail] if left else [hi, hi, lo, tail]
    return jnp.concatenate(blocks, axis=0)


def lanes(x, c):
    return jnp.broadcast_to(x[:, c : c + 1], (8, BLK))


def rows(x, j):
    return jnp.broadcast_to(x[j : j + 1, :], (8, BLK))


def reciprocal(p):
    return pl.reciprocal(p, approx=True)


def total(terms):
    while len(terms) > 1:
        terms = [terms[i] + terms[i + 1] for i in range(0, len(terms), 2)]
    return terms[0]


def factor_block(block):
    n = BLK // 8
    sub = lax.broadcasted_iota(jnp.int32, (8, BLK), 0)
    lane = lax.broadcasted_iota(jnp.int32, (8, BLK), 1)
    t = [block[8 * r : 8 * r + 8, :] for r in range(n)]
    s = [jnp.where(lane == sub + 8 * r, 1.0, 0.0).astype(F32) for r in range(n)]
    for k in range(n):
        top, side = t[k], s[k]
        v = [lanes(top, 8 * k + j) for j in range(8)]
        mult = []
        diag = jnp.ones((8, BLK), F32)
        for x in range(0, 8, 2):
            z = x + 1
            f = [rows(v[m], x) for m in range(8)]
            g = [rows(v[m], z) for m in range(8)]
            pa, pb, pc = f[x], f[z], g[z]
            det = pa * pc - pb * pb
            q = reciprocal(det)
            qa = reciprocal(pa)
            mult.append(jnp.where(sub > x, v[x] * qa, 0.0))
            mult.append(jnp.where(sub > z, (v[z] - v[x] * (pb * qa)) * (pa * q), 0.0))
            diag = jnp.where(sub == x, pa, jnp.where(sub == z, det * qa, diag))
            vx = jnp.where(sub == x, v[x] - 1.0, v[x])
            vz = jnp.where(sub == z, v[z] - 1.0, v[z])
            hx = pc * vx - pb * vz
            hz = pa * vz - pb * vx
            v = [
                jnp.where(sub == x, 1.0, 0.0) - hx * q
                if m == x
                else jnp.where(sub == z, 1.0, 0.0) - hz * q
                if m == z
                else v[m] - (hx * f[m] + hz * g[m]) * q
                for m in range(8)
            ]
        wt = total([v[j] * rows(top, j) for j in range(8)])
        ws = total([v[j] * rows(side, j) for j in range(8)])
        wtr = [rows(wt, j) for j in range(8)]
        wsr = [rows(ws, j) for j in range(8)]
        for r in range(k + 1, n):
            c = [lanes(t[r], 8 * k + j) for j in range(8)]
            t[r] = t[r] - total([c[j] * wtr[j] for j in range(8)])
            s[r] = s[r] - total([c[j] * wsr[j] for j in range(8)])
        for j in range(7):
            top = top - mult[j] * rows(top, j)
            side = side - mult[j] * rows(side, j)
        root = lax.rsqrt(diag)
        t[k] = jnp.where(lane >= sub + 8 * k, top * root, 0.0)
        s[k] = side * root
    return jnp.concatenate(t, axis=0), jnp.concatenate(s, axis=0)


def panel_kernel(
    share, pan_ref, look_ref, rows_ref, sc_ref, u_out, panel_out, ahead_out,
    lhs, a, uh, ul, ih, il, work, y, yh, yl, zh, zl,
):
    b = pan_ref.shape[1]
    n_blk = b // BLK
    wide = b + BLK
    col = lax.axis_index("col")
    first = col * share
    home = first // BLK
    scales = sc_ref[...]
    lhs[...] = stacked(pan_ref[...], scales, True).T.astype(BF16)
    look_lhs = stacked(look_ref[...], scales, True).T.astype(BF16)

    def entries(pts, e):
        return jnp.exp(dot(lhs[:e, :], stacked(pts, scales, False).astype(BF16)))

    for c in range(0, b, TILE):
        e = c + TILE
        at_row = lax.broadcasted_iota(jnp.int32, (e, TILE), 0)
        at_col = lax.broadcasted_iota(jnp.int32, (e, TILE), 1) + c
        a[:e, c:e] = entries(pan_ref[:, c:e], e) + jnp.where(at_row == at_col, RIDGE, 0.0)
    a[:, b:wide] = entries(look_ref[...], b)

    for i in range(n_blk):
        s = i * BLK
        e = s + BLK

        def current(lo, hi, s=s, e=e):
            cur = a[s:e, lo:hi]
            if s > 0:
                cur = cur - product(dot_t, uh[:s, s:e], ul[:s, s:e], uh[:s, lo:hi], ul[:s, lo:hi])
            return cur

        upper, inverse = factor_block(current(s, e))
        a[s:e, s:e] = upper
        inv_h, inv_l = split(inverse)
        ih[s:e, :] = inv_h
        il[s:e, :] = inv_l
        for lo, hi in ((e, e + BLK), (e + BLK, wide)):
            if lo < hi:
                rh, rl = split(current(lo, hi))
                done = product(dot, inv_h, inv_l, rh, rl)
                a[s:e, lo:hi] = done
                dh, dl = split(done)
                uh[s:e, lo:hi] = dh
                ul[s:e, lo:hi] = dl

    at_row = lax.broadcasted_iota(jnp.int32, (BLK, BLK), 0)
    at_col = lax.broadcasted_iota(jnp.int32, (BLK, BLK), 1)
    unit = jnp.where(at_row == at_col, 1.0, 0.0).astype(F32)
    for i in reversed(range(n_blk)):
        s = i * BLK
        right = jnp.concatenate([jnp.where(home == i, unit, 0.0), a[s : s + BLK, b:wide]], axis=1)
        if i < n_blk - 1:
            e = s + BLK
            right = right - product(dot, uh[s:e, e:b], ul[s:e, e:b], yh[e:, :], yl[e:, :])
        rh, rl = split(right)
        done = product(dot_t, ih[s : s + BLK, :], il[s : s + BLK, :], rh, rl)
        y[s : s + BLK, :] = done
        dh, dl = split(done)
        yh[s : s + BLK, :] = dh
        yl[s : s + BLK, :] = dl
    th, tl = split(y[...].T)
    zh[...] = th
    zl[...] = tl

    inner = pl.multiple_of(lax.rem(first, BLK), min(share, BLK))

    @pl.loop(0, rows_ref.shape[1] // TILE)
    def _(step):
        at = pl.ds(pl.multiple_of(step * TILE, TILE), TILE)
        pts = stacked(rows_ref[:, at], scales, False).astype(BF16)
        kh, kl = split(jnp.exp(dot(lhs[...], pts)))
        both = product(dot, zh[...], zl[...], kh, kl)
        ahead = jnp.exp(dot(look_lhs, pts)) - both[BLK:, :]
        if share == BLK:
            panel_out[:, at] = both[:BLK, :]
            ahead_out[:, at] = ahead
        else:
            work[:, :TILE] = both[:BLK, :]
            panel_out[:, at] = work[pl.ds(inner, share), :TILE]
            ahead_out[:, at] = ahead[:share, :]

    u_rows = u_out.shape[0] if share == BLK else u_out.shape[1]
    u_first = pl.multiple_of(lax.axis_index("row") * u_rows, BLK)
    u_tile = a[pl.ds(pl.multiple_of(first, share), share), pl.ds(u_first, u_rows)]
    if share == BLK:
        at_row = lax.broadcasted_iota(jnp.int32, (u_rows, share), 0) + u_first
        at_col = lax.broadcasted_iota(jnp.int32, (u_rows, share), 1) + first
        u_out[...] = jnp.where(at_row >= at_col, u_tile.T, 0.0)
    else:
        u_out[...] = u_tile


def panel_step(panel, look, row_points, scales, share, row_share):
    feats, b = panel.shape
    rows_dev = row_points.shape[1]
    wide = b + BLK
    vmem = pl.BlockSpec(memory_space=pltpu.VMEM)
    return pl.pallas_call(
        functools.partial(panel_kernel, share),
        out_shape=(
            jax.ShapeDtypeStruct((row_share, share) if share == BLK else (share, row_share), F32),
            jax.ShapeDtypeStruct((share, rows_dev), F32),
            jax.ShapeDtypeStruct((share, rows_dev), F32),
        ),
        in_specs=[vmem] * 4,
        out_specs=(vmem,) * 3,
        scratch_shapes=[
            pltpu.VMEM((b, 4 * feats), BF16),
            pltpu.VMEM((b, wide), F32),
            pltpu.VMEM((b, wide), BF16),
            pltpu.VMEM((b, wide), BF16),
            pltpu.VMEM((b, BLK), BF16),
            pltpu.VMEM((b, BLK), BF16),
            pltpu.VMEM((BLK, TILE), F32),
            pltpu.VMEM((b, 2 * BLK), F32),
            pltpu.VMEM((b, 2 * BLK), BF16),
            pltpu.VMEM((b, 2 * BLK), BF16),
            pltpu.VMEM((2 * BLK, b), BF16),
            pltpu.VMEM((2 * BLK, b), BF16),
        ],
        compiler_params=pltpu.CompilerParams(vmem_limit_bytes=48 * 1024 * 1024),
        name="panel_step",
    )(panel, look, row_points, scales[:, None])


def body(row_points, panel_points, scales):
    n_col = lax.axis_size("col")
    n_row = lax.axis_size("row")
    col_index = lax.axis_index("col")
    row_index = lax.axis_index("row")
    feats, share = panel_points.shape
    b = share * n_col
    row_share = b // n_row
    rows_dev = row_points.shape[1]
    assert b <= rows_dev and BLK % share == 0
    first_col = col_index * share
    if share == BLK:
        panel, look = gather_points(panel_points, row_points, n_row, n_col, 0)
        return panel_step(panel, look, row_points, scales, share, row_share)
    local_look = lax.dynamic_slice_in_dim(row_points, first_col, share, 1)
    gathered, look = gather_points(panel_points, local_look, n_row, n_col, 0)
    panel = jnp.transpose(gathered, (1, 0, 2)).reshape(feats, b)
    look = jnp.pad(look, ((0, 0), (0, BLK - share)))
    u_tile, panel_tile, updated = panel_step(panel, look, row_points, scales, share, row_share)
    at_row = lax.broadcasted_iota(jnp.int32, (row_share, share), 0) + row_index * row_share
    at_col = lax.broadcasted_iota(jnp.int32, (row_share, share), 1) + first_col
    diag_tile = jnp.where(at_row >= at_col, u_tile.T, 0.0)
    return (diag_tile, panel_tile, updated)


def solution(mesh):
    return jax.shard_map(
        body,
        mesh=mesh,
        in_specs=(P(None, "row"), P(None, "col"), P()),
        out_specs=(P("row", "col"), P("col", "row"), P("col", "row")),
        check_vma=False,
    )
```

```python
import functools

import jax
import jax.numpy as jnp
from jax import lax
from jax.experimental import pallas as pl
from jax.experimental.pallas import tpu as pltpu
from jax.sharding import PartitionSpec as P

RIDGE = 0.5
BLK = 128
TILE = 256
F32 = jnp.float32
BF16 = jnp.bfloat16


def gather_kernel(n_row, n_col, root, pan_ref, look_ref, g_ref, lk_ref, send, recv, lsend, lrecv, own):
    row = lax.axis_index("row")
    col = lax.axis_index("col")
    share = pan_ref.shape[1]
    aligned = share % BLK == 0

    def slot(c):
        if aligned:
            return g_ref.at[:, pl.ds(pl.multiple_of(c * share, share), share)]
        return g_ref.at[c]

    look_src = look_ref.at[:, pl.ds(pl.multiple_of(col * share, share), share)] if aligned else look_ref
    barrier = pltpu.get_barrier_semaphore()
    for d in range(1, n_col):
        pl.semaphore_signal(
            barrier, inc=1, device_id=(row, lax.rem(col + d, n_col)), device_id_type=pl.DeviceIdType.MESH
        )
    for d in range(1, n_row):
        pl.semaphore_signal(
            barrier, inc=1, device_id=(lax.rem(row + d, n_row), col), device_id_type=pl.DeviceIdType.MESH
        )
    pl.semaphore_wait(barrier, n_col + n_row - 2)

    def panel_copy(d):
        return pltpu.make_async_remote_copy(
            src_ref=pan_ref,
            dst_ref=slot(col),
            send_sem=send.at[d],
            recv_sem=recv.at[d],
            device_id=(row, lax.rem(col + d, n_col)),
            device_id_type=pl.DeviceIdType.MESH,
        )

    def panel_arrival(d):
        return pltpu.make_async_remote_copy(
            src_ref=pan_ref,
            dst_ref=slot(lax.rem(col + n_col - d, n_col)),
            send_sem=send.at[d],
            recv_sem=recv.at[d],
            device_id=(row, lax.rem(col + d, n_col)),
            device_id_type=pl.DeviceIdType.MESH,
        )

    def look_copy(d):
        return pltpu.make_async_remote_copy(
            src_ref=look_src,
            dst_ref=lk_ref,
            send_sem=lsend.at[d],
            recv_sem=lrecv,
            device_id=(lax.rem(row + d, n_row), col),
            device_id_type=pl.DeviceIdType.MESH,
        )

    @pl.when(row == root)
    def _():
        for d in range(1, n_row):
            look_copy(d).start()

    for d in range(1, n_col):
        panel_copy(d).start()
    mine = pltpu.make_async_copy(pan_ref, slot(col), own.at[0])
    mine.start()

    @pl.when(row == root)
    def _():
        keep = pltpu.make_async_copy(look_src, lk_ref, own.at[1])
        keep.start()
        keep.wait()
        for d in range(1, n_row):
            look_copy(d).wait_send()

    @pl.when(row != root)
    def _():
        look_copy(1).wait_recv()

    mine.wait()
    for d in range(1, n_col):
        panel_copy(d).wait_send()
        panel_arrival(d).wait_recv()


def gather_points(panel_points, local_look, n_row, n_col, root):
    feats, share = panel_points.shape
    vmem = pl.BlockSpec(memory_space=pltpu.VMEM)
    return pl.pallas_call(
        functools.partial(gather_kernel, n_row, n_col, root),
        out_shape=(
            jax.ShapeDtypeStruct((feats, n_col * share) if share % BLK == 0 else (n_col, feats, share), F32),
            jax.ShapeDtypeStruct((feats, share), F32),
        ),
        in_specs=[vmem, pl.BlockSpec(memory_space=pl.ANY) if share % BLK == 0 else vmem],
        out_specs=(vmem, vmem),
        scratch_shapes=[
            pltpu.SemaphoreType.DMA((n_col,)),
            pltpu.SemaphoreType.DMA((n_col,)),
            pltpu.SemaphoreType.DMA((n_row,)),
            pltpu.SemaphoreType.DMA,
            pltpu.SemaphoreType.DMA((2,)),
        ],
        compiler_params=pltpu.CompilerParams(collective_id=0, has_side_effects=True),
        name="gather_points",
    )(panel_points, local_look)


def split(x):
    hi = x.astype(BF16)
    return hi, (x - hi.astype(F32)).astype(BF16)


def parts3(x):
    a = x.astype(BF16).astype(F32)
    b = (x - a).astype(BF16).astype(F32)
    return a, b, (x - a) - b


def dot(a, b):
    return jnp.dot(a, b, preferred_element_type=F32)


def dot_t(a, b):
    return lax.dot_general(a, b, (((0,), (0,)), ((), ())), preferred_element_type=F32)


def product(mul, ah, al, bh, bl):
    return mul(ah, bh) + (mul(ah, bl) + mul(al, bh))


def stacked(points, scales, left):
    feats, n = points.shape
    weighted = points * scales
    norm = jnp.sum(weighted * points, axis=0, keepdims=True)
    main = 2.0 * weighted if left else points
    hi = main.astype(BF16).astype(F32)
    lo = main - hi
    n0, n1, n2 = (jnp.broadcast_to(-p, (feats, n)) for p in parts3(norm))
    place = lax.broadcasted_iota(jnp.int32, (feats, n), 0)
    first = 0 if left else 3
    ones = jnp.where((place >= 3 - first) & (place < 6 - first), 1.0, 0.0)
    tail = jnp.where(
        place == first, n0, jnp.where(place == first + 1, n1, jnp.where(place == first + 2, n2, ones))
    )
    blocks = [hi, lo, hi, tail] if left else [hi, hi, lo, tail]
    return jnp.concatenate(blocks, axis=0)


def lanes(x, c):
    return jnp.broadcast_to(x[:, c : c + 1], (8, BLK))


def rows(x, j):
    return jnp.broadcast_to(x[j : j + 1, :], (8, BLK))


def reciprocal(p):
    return pl.reciprocal(p, approx=True)


def total(terms):
    while len(terms) > 1:
        terms = [terms[i] + terms[i + 1] for i in range(0, len(terms), 2)]
    return terms[0]


def factor_block(block):
    n = BLK // 8
    sub = lax.broadcasted_iota(jnp.int32, (8, BLK), 0)
    lane = lax.broadcasted_iota(jnp.int32, (8, BLK), 1)
    t = [block[8 * r : 8 * r + 8, :] for r in range(n)]
    s = [jnp.where(lane == sub + 8 * r, 1.0, 0.0).astype(F32) for r in range(n)]
    for k in range(n):
        top, side = t[k], s[k]
        v = [lanes(top, 8 * k + j) for j in range(8)]
        mult = []
        diag = jnp.ones((8, BLK), F32)
        for x in range(0, 8, 2):
            z = x + 1
            f = [rows(v[m], x) for m in range(8)]
            g = [rows(v[m], z) for m in range(8)]
            pa, pb, pc = f[x], f[z], g[z]
            det = pa * pc - pb * pb
            q = reciprocal(det)
            qa = reciprocal(pa)
            mult.append(jnp.where(sub > x, v[x] * qa, 0.0))
            mult.append(jnp.where(sub > z, (v[z] - v[x] * (pb * qa)) * (pa * q), 0.0))
            diag = jnp.where(sub == x, pa, jnp.where(sub == z, det * qa, diag))
            vx = jnp.where(sub == x, v[x] - 1.0, v[x])
            vz = jnp.where(sub == z, v[z] - 1.0, v[z])
            hx = pc * vx - pb * vz
            hz = pa * vz - pb * vx
            v = [
                jnp.where(sub == x, 1.0, 0.0) - hx * q
                if m == x
                else jnp.where(sub == z, 1.0, 0.0) - hz * q
                if m == z
                else v[m] - (hx * f[m] + hz * g[m]) * q
                for m in range(8)
            ]
        wt = total([v[j] * rows(top, j) for j in range(8)])
        ws = total([v[j] * rows(side, j) for j in range(8)])
        wtr = [rows(wt, j) for j in range(8)]
        wsr = [rows(ws, j) for j in range(8)]
        for r in range(k + 1, n):
            c = [lanes(t[r], 8 * k + j) for j in range(8)]
            t[r] = t[r] - total([c[j] * wtr[j] for j in range(8)])
            s[r] = s[r] - total([c[j] * wsr[j] for j in range(8)])
        for j in range(7):
            top = top - mult[j] * rows(top, j)
            side = side - mult[j] * rows(side, j)
        root = lax.rsqrt(diag)
        t[k] = jnp.where(lane >= sub + 8 * k, top * root, 0.0)
        s[k] = side * root
    return jnp.concatenate(t, axis=0), jnp.concatenate(s, axis=0)


def panel_kernel(
    share, pan_ref, look_ref, rows_ref, sc_ref, u_out, panel_out, ahead_out,
    lhs, a, uh, ul, ih, il, work, y, yh, yl, zh, zl, kh, kl,
):
    b = pan_ref.shape[1]
    n_blk = b // BLK
    wide = b + BLK
    col = lax.axis_index("col")
    first = col * share
    home = first // BLK
    feats = sc_ref.shape[1]
    f_row = lax.broadcasted_iota(jnp.int32, (feats, feats), 0)
    f_col = lax.broadcasted_iota(jnp.int32, (feats, feats), 1)
    scales = jnp.sum(jnp.where(f_row == f_col, sc_ref[...], 0.0), axis=1, keepdims=True)
    lhs[...] = stacked(pan_ref[...], scales, True).T.astype(BF16)
    look_lhs = stacked(look_ref[...], scales, True).T.astype(BF16)

    def entries(pts, e):
        return jnp.exp(dot(lhs[:e, :], stacked(pts, scales, False).astype(BF16)))

    for c in range(0, b, TILE):
        e = c + TILE
        at_row = lax.broadcasted_iota(jnp.int32, (e, TILE), 0)
        at_col = lax.broadcasted_iota(jnp.int32, (e, TILE), 1) + c
        a[:e, c:e] = entries(pan_ref[:, c:e], e) + jnp.where(at_row == at_col, RIDGE, 0.0)
    a[:, b:wide] = entries(look_ref[...], b)

    for i in range(n_blk):
        s = i * BLK
        e = s + BLK

        def current(lo, hi, s=s, e=e):
            cur = a[s:e, lo:hi]
            if s > 0:
                cur = cur - product(dot_t, uh[:s, s:e], ul[:s, s:e], uh[:s, lo:hi], ul[:s, lo:hi])
            return cur

        upper, inverse = factor_block(current(s, e))
        for c in range(i * TILE, rows_ref.shape[1], n_blk * TILE):
            pts = stacked(rows_ref[:, c : c + TILE], scales, False).astype(BF16)
            eh, el = split(jnp.exp(dot(lhs[...], pts)))
            kh[:, c : c + TILE] = eh
            kl[:, c : c + TILE] = el
            ahead_out[:, c : c + TILE] = jnp.exp(dot(look_lhs, pts))[:share, :]
        a[s:e, s:e] = upper
        inv_h, inv_l = split(inverse)
        ih[s:e, :] = inv_h
        il[s:e, :] = inv_l
        for lo, hi in ((e, e + BLK), (e + BLK, wide)):
            if lo < hi:
                rh, rl = split(current(lo, hi))
                done = product(dot, inv_h, inv_l, rh, rl)
                a[s:e, lo:hi] = done
                dh, dl = split(done)
                uh[s:e, lo:hi] = dh
                ul[s:e, lo:hi] = dl

    at_row = lax.broadcasted_iota(jnp.int32, (BLK, BLK), 0)
    at_col = lax.broadcasted_iota(jnp.int32, (BLK, BLK), 1)
    unit = jnp.where(at_row == at_col, 1.0, 0.0).astype(F32)
    for i in reversed(range(n_blk)):
        s = i * BLK
        right = jnp.concatenate([jnp.where(home == i, unit, 0.0), a[s : s + BLK, b:wide]], axis=1)
        if i < n_blk - 1:
            e = s + BLK
            right = right - product(dot, uh[s:e, e:b], ul[s:e, e:b], yh[e:, :], yl[e:, :])
        rh, rl = split(right)
        done = product(dot_t, ih[s : s + BLK, :], il[s : s + BLK, :], rh, rl)
        y[s : s + BLK, :] = done
        dh, dl = split(done)
        yh[s : s + BLK, :] = dh
        yl[s : s + BLK, :] = dl
    th, tl = split(y[...].T)
    zh[...] = th
    zl[...] = tl

    inner = pl.multiple_of(lax.rem(first, BLK), min(share, BLK))

    @pl.loop(0, rows_ref.shape[1] // TILE)
    def _(step):
        at = pl.ds(pl.multiple_of(step * TILE, TILE), TILE)
        both = product(dot, zh[...], zl[...], kh[:, at], kl[:, at])
        ahead_out[:, at] -= both[BLK : BLK + share, :]
        if share == BLK:
            panel_out[:, at] = both[:BLK, :]
        else:
            work[:, :TILE] = both[:BLK, :]
            panel_out[:, at] = work[pl.ds(inner, share), :TILE]

    u_rows = u_out.shape[0] if share == BLK else u_out.shape[1]
    u_first = pl.multiple_of(lax.axis_index("row") * u_rows, BLK)
    u_tile = a[pl.ds(pl.multiple_of(first, share), share), pl.ds(u_first, u_rows)]
    if share == BLK:
        at_row = lax.broadcasted_iota(jnp.int32, (u_rows, share), 0) + u_first
        at_col = lax.broadcasted_iota(jnp.int32, (u_rows, share), 1) + first
        u_out[...] = jnp.where(at_row >= at_col, u_tile.T, 0.0)
    else:
        u_out[...] = u_tile


def panel_step(panel, look, row_points, scales, share, row_share):
    feats, b = panel.shape
    rows_dev = row_points.shape[1]
    wide = b + BLK
    vmem = pl.BlockSpec(memory_space=pltpu.VMEM)
    return pl.pallas_call(
        functools.partial(panel_kernel, share),
        out_shape=(
            jax.ShapeDtypeStruct((row_share, share) if share == BLK else (share, row_share), F32),
            jax.ShapeDtypeStruct((share, rows_dev), F32),
            jax.ShapeDtypeStruct((share, rows_dev), F32),
        ),
        in_specs=[vmem] * 4,
        out_specs=(vmem,) * 3,
        scratch_shapes=[
            pltpu.VMEM((b, 4 * feats), BF16),
            pltpu.VMEM((b, wide), F32),
            pltpu.VMEM((b, wide), BF16),
            pltpu.VMEM((b, wide), BF16),
            pltpu.VMEM((b, BLK), BF16),
            pltpu.VMEM((b, BLK), BF16),
            pltpu.VMEM((BLK, TILE), F32),
            pltpu.VMEM((b, 2 * BLK), F32),
            pltpu.VMEM((b, 2 * BLK), BF16),
            pltpu.VMEM((b, 2 * BLK), BF16),
            pltpu.VMEM((2 * BLK, b), BF16),
            pltpu.VMEM((2 * BLK, b), BF16),
            pltpu.VMEM((b, rows_dev), BF16),
            pltpu.VMEM((b, rows_dev), BF16),
        ],
        compiler_params=pltpu.CompilerParams(vmem_limit_bytes=48 * 1024 * 1024),
        name="panel_step",
    )(panel, look, row_points, scales[None, :])


def body(row_points, panel_points, scales):
    n_col = lax.axis_size("col")
    n_row = lax.axis_size("row")
    col_index = lax.axis_index("col")
    row_index = lax.axis_index("row")
    feats, share = panel_points.shape
    b = share * n_col
    row_share = b // n_row
    rows_dev = row_points.shape[1]
    assert b <= rows_dev and BLK % share == 0
    first_col = col_index * share
    if share == BLK:
        panel, look = gather_points(panel_points, row_points, n_row, n_col, 0)
        return panel_step(panel, look, row_points, scales, share, row_share)
    local_look = lax.dynamic_slice_in_dim(row_points, first_col, share, 1)
    gathered, look = gather_points(panel_points, local_look, n_row, n_col, 0)
    panel = jnp.transpose(gathered, (1, 0, 2)).reshape(feats, b)
    look = jnp.pad(look, ((0, 0), (0, BLK - share)))
    u_tile, panel_tile, updated = panel_step(panel, look, row_points, scales, share, row_share)
    at_row = lax.broadcasted_iota(jnp.int32, (row_share, share), 0) + row_index * row_share
    at_col = lax.broadcasted_iota(jnp.int32, (row_share, share), 1) + first_col
    diag_tile = jnp.where(at_row >= at_col, u_tile.T, 0.0)
    return (diag_tile, panel_tile, updated)


def solution(mesh):
    return jax.shard_map(
        body,
        mesh=mesh,
        in_specs=(P(None, "row"), P(None, "col"), P()),
        out_specs=(P("row", "col"), P("col", "row"), P("col", "row")),
        check_vma=False,
    )
```
